128 devices in a mesh: ctx: 32 (over y, x, z_hi), head: 4 (over z_lo, core).
Axes of the slice: x: 4, y: 4, z: 4 (z_hi: 2, z_lo: 2; z = z_hi * 2 + z_lo), core: 2. Of those that a mesh axis runs over, the one named last changes fastest.
Arguments:
- queries: bfloat16 [12288, 8192], P('ctx', 'head'), parts along dimension 1, may hold values from -6 to 6
- key_rows: bfloat16 [12288, 512], P('ctx', 'head'), parts along dimension 1, may hold values from -6 to 6
- value_rows: bfloat16 [12288, 512], P('ctx', 'head'), parts along dimension 1, may hold values from -6 to 6
- out_grad: bfloat16 [12288, 8192], P('ctx', 'head'), parts along dimension 1, may hold values from -6 to 6
- partner: int32 [32, 4], replicated, may hold values from 0 to 31, as said below
- stripes: int32 [96], replicated, may hold values from 0 to 95, each once
Outputs:
- query_grad: bfloat16 [12288, 8192], P('ctx', 'head'), parts along dimension 1
- key_grad: bfloat16 [12288, 512], P('ctx', 'head'), parts along dimension 1
- value_grad: bfloat16 [12288, 512], P('ctx', 'head'), parts along dimension 1
The draws below stay inside these ranges and needn't reach their ends.
There are 4 independent parts, one for each index of `head`. The reference program is written for one: setup_inputs(seed, part) draws one part's arguments, and reference() takes and returns one part's arrays. A program takes and returns all parts, laid end to end along the dimension named above; an argument that names none is the same for every part. Nothing has to cross between parts.
Inputs may be any that keep to these rules, and one draw needn't show every extreme that they name: partner[i, r] = i XOR m_r for 4 distinct nonzero round masks m_r, one of which is 16, so each round pairs the indices of ctx two by two.
All inputs are finite; a program needn't handle non-finite values.
Results may differ from the reference program's by a relative error of at most 0.0064.
Values may be sent and summed in bfloat16 or wider, within the bound.
A program may use at most 256 MiB of HBM per device.

```python
import math
import jax
import jax.numpy as jnp
from jax import lax

H = 16
E = 128
BLK = 128
BPD = 3
ROUNDS = 4
TOK_DEV = 384
TOKENS = 12288
BLOCKS = 96
N_CTX = 32


def draw_key_rows(key, part):
    key = jax.random.fold_in(key, 11)
    drawn = jnp.clip(jax.random.normal(key, (TOKENS, E)), -6.0, 6.0)
    return drawn.astype(jnp.bfloat16)


def draw_queries(key, part):
    key = jax.random.fold_in(key, 12)
    drawn = jnp.clip(jax.random.normal(key, (TOKENS, H * E)), -6.0, 6.0)
    return drawn.astype(jnp.bfloat16)


def draw_partner(key, part):
    key = jax.random.fold_in(key, 21)
    candidates = jax.random.permutation(key, N_CTX - 1).astype(jnp.int32) + 1
    placing = jnp.where(candidates == N_CTX // 2, -1, jnp.arange(N_CTX - 1, dtype=jnp.int32))
    ordered = candidates[jnp.argsort(placing, stable=True)][:ROUNDS]
    turn = jax.random.randint(jax.random.fold_in(key, 5), (), 0, ROUNDS)
    round_masks = jnp.roll(ordered, turn)
    indices = jnp.arange(N_CTX, dtype=jnp.int32)
    return jnp.bitwise_xor(indices[:, None], round_masks[None, :].astype(jnp.int32)).astype(jnp.int32)


def levels(stream_key, dims, pieces, low, largest):
    def one(dim, blocks):
        draws = jax.random.uniform(jax.random.fold_in(jax.random.fold_in(stream_key, 6), dim), (blocks,), jnp.float32, low / len(pieces), largest / len(pieces))
        return jnp.repeat(jnp.exp(draws), dims[dim] // blocks).reshape((-1,) + (1,) * (len(dims) - dim - 1))

    level = one(*pieces[0])
    for cut in pieces[1:]:
        level = level * one(*cut)
    return level


def centred(rng, shape, deviation, bound, cuts=(), kind=jnp.bfloat16):
    entries = jax.random.normal(rng, shape, jnp.float32) * deviation
    if len(cuts) > 0:
        entries = levels(rng, shape, cuts, -0.22, 0.18) * entries
    return jnp.clip(entries, min=-bound, max=bound).astype(kind)


def setup_inputs(seed: int = 0, part: int = 0) -> dict:
    splits = jax.random.split(jax.random.key(seed), 7)
    part_keys = jax.random.split(jax.random.fold_in(splits[6], part), 7)
    queries = draw_queries(jax.random.fold_in(jax.random.fold_in(splits[6], part), 71), part)
    key_rows = draw_key_rows(jax.random.fold_in(jax.random.fold_in(splits[6], part), 71), part)
    value_rows = centred(part_keys[2], (TOKENS, E), 1.0, 6.0, ((0, 32),))
    out_grad = centred(part_keys[3], (TOKENS, H * E), 1.0, 6.0, ((0, 32),))
    partner = draw_partner(jax.random.fold_in(splits[6], 71), part)
    stripes = jax.random.permutation(splits[5], BLOCKS).astype(jnp.int32)
    return {"queries": queries, "key_rows": key_rows, "value_rows": value_rows, "out_grad": out_grad, "partner": partner, "stripes": stripes}


def token_places(stripes, device):
    owned_blocks = lax.dynamic_slice_in_dim(stripes, device * BPD, BPD)
    within = jnp.arange(TOK_DEV, dtype=jnp.int32)
    return jnp.repeat(owned_blocks, BLK, total_repeat_length=TOK_DEV) * BLK + within % BLK

def reference(queries, key_rows, value_rows, out_grad, partner, stripes):
    score_scale = 1.0 / math.sqrt(E)
    query_dev = queries.reshape(N_CTX, TOK_DEV, H, E)
    grad_dev = out_grad.reshape(N_CTX, TOK_DEV, H, E)
    key_dev = key_rows.reshape(N_CTX, TOK_DEV, E)
    value_dev = value_rows.reshape(N_CTX, TOK_DEV, E)

    def one_device(running, device):
        key_acc, value_acc = running
        sources = jnp.concatenate([device[None], partner[device]]).astype(jnp.int32)
        here_keys = key_dev[sources].reshape(-1, E).astype(jnp.float32)
        here_values = value_dev[sources].reshape(-1, E).astype(jnp.float32)
        key_places = jax.vmap(lambda source: token_places(stripes, source))(sources).reshape(-1)
        query_places = token_places(stripes, device)
        allowed = key_places[None, :] <= query_places[:, None]
        query_now = query_dev[device].astype(jnp.float32)
        grad_now = grad_dev[device].astype(jnp.float32)
        scores = jnp.einsum('thd,sd->hts', query_now, here_keys) * score_scale
        scores = jnp.where(allowed[None], scores, -jnp.inf)
        row_max = lax.optimization_barrier(jnp.max(scores, axis=-1, keepdims=True))
        raised = jnp.exp(scores - row_max)
        row_sum = lax.optimization_barrier(jnp.sum(raised, axis=-1, keepdims=True))
        probs = raised / row_sum
        prob_grad = jnp.einsum('thd,sd->hts', grad_now, here_values)
        row_delta = lax.optimization_barrier(jnp.sum(probs * prob_grad, axis=-1, keepdims=True))
        score_low = (score_scale * probs * (prob_grad - row_delta)).astype(jnp.bfloat16)
        probs_low = probs.astype(jnp.bfloat16)
        score_low = lax.optimization_barrier(score_low)
        probs_low = lax.optimization_barrier(probs_low)
        score_grad = score_low.astype(jnp.float32)
        probs_back = probs_low.astype(jnp.float32)
        query_out = jnp.einsum('hts,sd->thd', score_grad, here_keys)
        key_part = jnp.einsum('hts,thd->sd', score_grad, query_now).reshape(ROUNDS + 1, TOK_DEV, E)
        value_part = jnp.einsum('hts,thd->sd', probs_back, grad_now).reshape(ROUNDS + 1, TOK_DEV, E)
        key_acc = key_acc.at[sources].add(key_part)
        value_acc = value_acc.at[sources].add(value_part)
        return ((key_acc, value_acc), query_out.reshape(TOK_DEV, H * E).astype(jnp.bfloat16))
    zeros_start = jnp.zeros((N_CTX, TOK_DEV, E), jnp.float32)
    (key_acc, value_acc), query_grad = lax.scan(one_device, (zeros_start, zeros_start), jnp.arange(N_CTX, dtype=jnp.int32))
    return (query_grad.reshape(TOKENS, H * E), key_acc.reshape(TOKENS, E).astype(jnp.bfloat16), value_acc.reshape(TOKENS, E).astype(jnp.bfloat16))
```

```python
import functools
import math

import jax
import jax.numpy as jnp
from jax import lax
from jax.experimental import pallas as pl
from jax.experimental.pallas import tpu as pltpu
from jax.sharding import PartitionSpec as P

HEADS = 16
WIDTH = 128
BLOCK = 128
OWNED = 3
ROUNDS = 4
ROWS = OWNED * BLOCK
KEY_BLOCKS = OWNED * (ROUNDS + 1)
PAIRS = (KEY_BLOCKS + 1) // 2
SCALE = 1.0 / math.sqrt(WIDTH)
SCALE_LOG2 = SCALE * math.log2(math.e)
F32 = jnp.float32
BF16 = jnp.bfloat16
NT = (((1,), (1,)), ((), ()))


def attend_kernel(
    meta_ref, q_ref, do_ref, kv0, kv1, kv2, kv3, kv4,
    dq_ref, g0, g1, g2, g3, g4,
    kc, vc, kt, s_scr, dp_scr, p_scr, ds_scr, dk_acc, dv_acc, total, count, order,
):
    kvs = (kv0, kv1, kv2, kv3, kv4)
    grads = (g0, g1, g2, g3, g4)
    total[...] = jnp.zeros_like(total)

    def put(ref, start, slot):
        rows = pl.ds(pl.multiple_of(slot * BLOCK, BLOCK), BLOCK)
        src = pl.ds(start, BLOCK)
        k = ref[src, :WIDTH]
        kc[rows, :] = k
        vc[rows, :] = ref[src, WIDTH:]
        kt[:, rows] = k.T

    def query_block(a, _):
        place = meta_ref[a]
        here = pl.ds(pl.multiple_of(a * BLOCK, BLOCK), BLOCK)
        put(kv0, pl.multiple_of(a * BLOCK, BLOCK), 0)
        order[0] = a
        count[0] = 1
        for j in range(KEY_BLOCKS):
            @pl.when(meta_ref[j] < place)
            def _():
                slot = count[0]
                put(kvs[j // OWNED], (j % OWNED) * BLOCK, slot)
                order[slot] = j
                count[0] = slot + 1
        n = count[0]
        pairs = (n + 1) // 2
        odd = lax.rem(n, 2) == 1
        pad_bias = jnp.where(odd, -1e30, 0.0).astype(F32)

        @pl.when(odd)
        def _():
            rows = pl.ds(pl.multiple_of(n * BLOCK, BLOCK), BLOCK)
            kc[rows, :] = jnp.zeros((BLOCK, WIDTH), BF16)
            vc[rows, :] = jnp.zeros((BLOCK, WIDTH), BF16)
            kt[:, rows] = jnp.zeros((WIDTH, BLOCK), BF16)

        def zero(i, _):
            rows = pl.ds(pl.multiple_of(i * 2 * BLOCK, 2 * BLOCK), 2 * BLOCK)
            dk_acc[rows, :] = jnp.zeros((2 * BLOCK, WIDTH), F32)
            dv_acc[rows, :] = jnp.zeros((2 * BLOCK, WIDTH), F32)
            return 0

        lax.fori_loop(0, pairs, zero, 0)

        def two_heads(hp, _, k):
            def heads(ref):
                return jnp.concatenate(
                    [ref[here, pl.ds(pl.multiple_of(hp * 256 + o, 128), 128)] for o in (0, 128)], axis=0
                )

            q2, do2 = heads(q_ref), heads(do_ref)
            top = jnp.full((8, 256), -1e30, F32)
            for c in range(k):
                rows = pl.ds(c * 256, 256)
                s = lax.dot_general(kc[rows, :], q2, NT, preferred_element_type=F32)
                lo, hi = s[:128], s[128:]
                if c == 0:
                    key = lax.broadcasted_iota(jnp.int32, (128, 256), 0)
                    query = lax.broadcasted_iota(jnp.int32, (128, 256), 1) % 128
                    lo = jnp.where(key <= query, lo, -1e30)
                if c == k - 1:
                    hi = hi + pad_bias
                s = jnp.concatenate([lo, hi], axis=0)
                s_scr[rows, :] = s
                top = jnp.maximum(top, jnp.max(s.reshape(32, 8, 256), axis=0))
            top = jnp.max(top, axis=0, keepdims=True)
            norm = jnp.zeros((8, 256), F32)
            weighted = jnp.zeros((8, 256), F32)
            for c in range(k):
                rows = pl.ds(c * 256, 256)
                p = jnp.exp2((s_scr[rows, :] - top) * SCALE_LOG2)
                dp = lax.dot_general(vc[rows, :], do2, NT, preferred_element_type=F32)
                norm += jnp.sum(p.reshape(32, 8, 256), axis=0)
                weighted += jnp.sum((p * dp).reshape(32, 8, 256), axis=0)
                p_scr[rows, :] = p.astype(BF16)
                dp_scr[rows, :] = dp
            inverse = 1.0 / jnp.sum(norm, axis=0, keepdims=True)
            delta = jnp.sum(weighted, axis=0, keepdims=True) * inverse
            for c in range(k):
                rows = pl.ds(c * 256, 256)
                ds = p_scr[rows, :].astype(F32) * (dp_scr[rows, :] - delta)
                ds_scr[rows, :] = ds.astype(BF16)
            column = jnp.transpose(jnp.broadcast_to(inverse, (128, 256)))
            q_low = (q2.astype(F32) * (column * SCALE)).astype(BF16)
            do_low = (do2.astype(F32) * column).astype(BF16)
            for c in range(k):
                rows = pl.ds(c * 256, 256)
                dk_acc[rows, :] += jnp.dot(ds_scr[rows, :], q_low, preferred_element_type=F32)
                dv_acc[rows, :] += jnp.dot(p_scr[rows, :], do_low, preferred_element_type=F32)
            dqt = jnp.dot(kt[:, : k * 256], ds_scr[: k * 256, :], preferred_element_type=F32)
            dqt = dqt * (inverse * SCALE)
            for o in (0, 128):
                dq_ref[here, pl.ds(pl.multiple_of(hp * 256 + o, 128), 128)] = dqt[:, o : o + 128].T.astype(BF16)
            return 0

        for k in range(1, PAIRS + 1):
            @pl.when(pairs == k)
            def _():
                lax.fori_loop(0, HEADS // 2, functools.partial(two_heads, k=k), 0)

        def give(i, _):
            src = pl.ds(pl.multiple_of(i * BLOCK, BLOCK), BLOCK)
            dst = pl.ds(pl.multiple_of(order[i] * BLOCK, BLOCK), BLOCK)
            total[dst, :WIDTH] += dk_acc[src, :]
            total[dst, WIDTH:] += dv_acc[src, :]
            return 0

        lax.fori_loop(0, n, give, 0)
        return 0

    lax.fori_loop(0, OWNED, query_block, 0)
    for s in range(ROUNDS + 1):
        grads[s][...] = total[s * ROWS : (s + 1) * ROWS, :].astype(grads[s].dtype)


def attend(meta, q, do, kvs):
    vmem = pl.BlockSpec(memory_space=pltpu.VMEM)
    keys = 2 * BLOCK * PAIRS
    return pl.pallas_call(
        attend_kernel,
        out_shape=[jax.ShapeDtypeStruct(q.shape, BF16), jax.ShapeDtypeStruct((ROWS, 2 * WIDTH), F32)]
        + [jax.ShapeDtypeStruct((ROWS, 2 * WIDTH), BF16)] * ROUNDS,
        in_specs=[pl.BlockSpec(memory_space=pltpu.SMEM)] + [vmem] * 7,
        out_specs=[vmem] * 6,
        scratch_shapes=[
            pltpu.VMEM((keys, WIDTH), BF16),
            pltpu.VMEM((keys, WIDTH), BF16),
            pltpu.VMEM((WIDTH, keys), BF16),
            pltpu.VMEM((keys, 256), F32),
            pltpu.VMEM((keys, 256), F32),
            pltpu.VMEM((keys, 256), BF16),
            pltpu.VMEM((keys, 256), BF16),
            pltpu.VMEM((keys, WIDTH), F32),
            pltpu.VMEM((keys, WIDTH), F32),
            pltpu.VMEM((KEY_BLOCKS * BLOCK, 2 * WIDTH), F32),
            pltpu.SMEM((1,), jnp.int32),
            pltpu.SMEM((KEY_BLOCKS + 1,), jnp.int32),
        ],
        compiler_params=pltpu.CompilerParams(vmem_limit_bytes=48 * 1024 * 1024),
    )(meta, q, do, *kvs)


def exchange(mask, devices, arrays):
    def by(m):
        return lambda xs: tuple(lax.ppermute(x, "ctx", [(i, i ^ m) for i in range(devices)]) for x in xs)

    return lax.switch(mask - 1, [by(m) for m in range(1, devices)], arrays)


def local(queries, key_rows, value_rows, out_grad, partner, stripes):
    devices = lax.axis_size("ctx")
    device = lax.axis_index("ctx")
    masks = partner[0]
    payload = jnp.concatenate([key_rows, value_rows], axis=1)
    kvs = [payload]
    for r in range(ROUNDS):
        kvs += exchange(masks[r], devices, (payload,))
    sources = jnp.concatenate([device[None], partner[device]])
    meta = stripes.reshape(devices, OWNED)[sources].reshape(-1)
    dq, own, *parts = attend(meta, queries, out_grad, kvs)
    for r in range(ROUNDS):
        own = own + exchange(masks[r], devices, (parts[r],))[0].astype(F32)
    own = own.astype(BF16)
    return dq, own[:, :WIDTH], own[:, WIDTH:]


def solution(mesh):
    return jax.shard_map(
        local,
        mesh=mesh,
        in_specs=(P("ctx", "head"), P("ctx", "head"), P("ctx", "head"), P("ctx", "head"), P(), P()),
        out_specs=(P("ctx", "head"), P("ctx", "head"), P("ctx", "head")),
        check_vma=False,
    )
```

```python
import functools
import math

import jax
import jax.numpy as jnp
from jax import lax
from jax.experimental import pallas as pl
from jax.experimental.pallas import tpu as pltpu
from jax.sharding import PartitionSpec as P

HEADS = 16
GROUP = 4
WIDTH = 128
BLOCK = 128
OWNED = 3
ROUNDS = 4
ROWS = OWNED * BLOCK
KEY_BLOCKS = OWNED * (ROUNDS + 1)
SCALE = 1.0 / math.sqrt(WIDTH)
SCALE_LOG2 = SCALE * math.log2(math.e)
MESH = pl.DeviceIdType.MESH
F32 = jnp.float32
BF16 = jnp.bfloat16
NT = (((1,), (1,)), ((), ()))


def attend_kernel(
    order_ref, stripes_ref, q_ref, do_ref, kv0, kv1, kv2, kv3, kv4,
    dq_ref, g0, g1, g2, g3, g4,
    kc, vc, kt, bias, s_scr, dp_scr, p_scr, dqt, total, count, order,
):
    kvs = (kv0, kv1, kv2, kv3, kv4)
    grads = (g0, g1, g2, g3, g4)
    a = pl.program_id(0)
    device = lax.axis_index("ctx")
    cols = GROUP * BLOCK
    groups = HEADS // GROUP
    keys = kc.shape[0]

    def place_of(j):
        return stripes_ref[(device ^ order_ref[j // OWNED]) * OWNED + j % OWNED]

    @pl.when(a == 0)
    def _():
        total[...] = jnp.zeros_like(total)
        bias[...] = jnp.zeros_like(bias)
        key = lax.broadcasted_iota(jnp.int32, (BLOCK, BLOCK), 0)
        query = lax.broadcasted_iota(jnp.int32, (BLOCK, BLOCK), 1)
        bias[:BLOCK, :] = jnp.where(key <= query, 0.0, -1e30)

    def block(i):
        return pl.ds(pl.multiple_of(i * BLOCK, BLOCK), BLOCK)

    def put(ref, start, slot):
        src = pl.ds(start, BLOCK)
        k = ref[src, :WIDTH]
        kc[block(slot), :] = k
        vc[block(slot), :] = ref[src, WIDTH:]
        kt[:, block(slot)] = k.T

    place = stripes_ref[device * OWNED + a]
    put(kv0, pl.multiple_of(a * BLOCK, BLOCK), 0)
    order[0] = a
    count[0] = 1
    for j in range(KEY_BLOCKS):
        @pl.when(place_of(j) < place)
        def _():
            slot = count[0]
            put(kvs[j // OWNED], (j % OWNED) * BLOCK, slot)
            order[slot] = j
            count[0] = slot + 1
    n = count[0]
    odd = lax.rem(n, 2) == 1
    chunks = (n + 1) // 2

    @pl.when(odd)
    def _():
        kc[block(n), :] = jnp.zeros((BLOCK, WIDTH), BF16)
        vc[block(n), :] = jnp.zeros((BLOCK, WIDTH), BF16)
        kt[:, block(n)] = jnp.zeros((WIDTH, BLOCK), BF16)
        bias[block(n), :] = jnp.full((BLOCK, BLOCK), -1e30, F32)
        order[n] = KEY_BLOCKS

    def heads(ref, g):
        return jnp.concatenate([ref[:, block(g * GROUP + h)] for h in range(GROUP)], axis=0)

    def fold(x, op):
        return op(x.reshape(x.shape[0] // 8, 8, cols), axis=0)

    def run(first, second, third, top, inverse, delta):
        def chunk(c, carry):
            high, norm, weighted = carry
            rows = pl.ds(pl.multiple_of(c * 256, 256), 256)

            def at(g):
                return pl.ds(pl.multiple_of(lax.rem(g, 2) * keys + c * 256, 256), 256)

            if third is not None:
                p = p_scr[at(third), :] * inverse
                ds = (p * (dp_scr[at(third), :] - delta)).astype(BF16)
                low = p.astype(BF16)
                dk = jnp.dot(ds, heads(q_ref, third), preferred_element_type=F32)
                dv = jnp.dot(low, heads(do_ref, third), preferred_element_type=F32)
                for half in range(2):
                    here, part = block(order[2 * c + half]), slice(half * BLOCK, half * BLOCK + BLOCK)
                    total[here, :WIDTH] += dk[part]
                    total[here, WIDTH:] += dv[part]
                mine = pl.ds(pl.multiple_of(third * cols, cols), cols)
                dqt[:, mine] += jnp.dot(kt[:, rows], ds, preferred_element_type=F32)
            if second is not None:
                p = jnp.exp2((s_scr[at(second), :] - top) * SCALE_LOG2)
                dp = lax.dot_general(vc[rows, :], heads(do_ref, second), NT, preferred_element_type=F32)
                norm += fold(p, jnp.sum)
                weighted += fold(p * dp, jnp.sum)
                p_scr[at(second), :] = p
                dp_scr[at(second), :] = dp
            if first is not None:
                s = lax.dot_general(kc[rows, :], heads(q_ref, first), NT, preferred_element_type=F32)
                s += jnp.concatenate([bias[rows, :]] * GROUP, axis=1)
                high = jnp.maximum(high, fold(s, jnp.max))
                s_scr[at(first), :] = s
            return high, norm, weighted

        zero = jnp.zeros((8, cols), F32)
        high, norm, weighted = lax.fori_loop(0, chunks, chunk, (jnp.full((8, cols), -1e30, F32), zero, zero))
        inverse = 1.0 / jnp.sum(norm, axis=0, keepdims=True)
        return jnp.max(high, axis=0, keepdims=True), inverse, jnp.sum(weighted, axis=0, keepdims=True) * inverse

    dqt[...] = jnp.zeros_like(dqt)
    stats = run(0, None, None, None, None, None)
    stats = run(1, 0, None, stats[0], None, None)
    stats = lax.fori_loop(2, groups, lambda g, stats: run(g, g - 1, g - 2, *stats), stats)
    stats = run(None, groups - 1, groups - 2, *stats)
    run(None, None, groups - 1, *stats)
    for h in range(HEADS):
        here = slice(h * WIDTH, h * WIDTH + WIDTH)
        dq_ref[:, here] = (dqt[:, here] * SCALE).astype(BF16).T

    @pl.when(odd)
    def _():
        bias[block(n), :] = jnp.zeros((BLOCK, BLOCK), F32)

    @pl.when(a == OWNED - 1)
    def _():
        for s in range(ROUNDS + 1):
            rows = slice(s * ROWS, (s + 1) * ROWS)
            grads[s][:, :WIDTH] = (total[rows, :WIDTH] * SCALE).astype(grads[s].dtype)
            grads[s][:, WIDTH:] = total[rows, WIDTH:].astype(grads[s].dtype)


def attend(order, stripes, q, do, kvs):
    smem = pl.BlockSpec(memory_space=pltpu.SMEM)
    part = pl.BlockSpec((ROWS, 2 * WIDTH), lambda a: (0, 0))
    rows = pl.BlockSpec((BLOCK, HEADS * WIDTH), lambda a: (a, 0))
    keys = (KEY_BLOCKS + 1) * BLOCK
    cols = GROUP * BLOCK
    return pl.pallas_call(
        attend_kernel,
        out_shape=[jax.ShapeDtypeStruct(q.shape, BF16), jax.ShapeDtypeStruct((ROWS, 2 * WIDTH), F32)]
        + [jax.ShapeDtypeStruct((ROWS, 2 * WIDTH), BF16)] * ROUNDS,
        grid=(OWNED,),
        in_specs=[smem, smem, rows, rows] + [part] * (ROUNDS + 1),
        out_specs=[rows] + [part] * (ROUNDS + 1),
        scratch_shapes=[
            pltpu.VMEM((keys, WIDTH), BF16),
            pltpu.VMEM((keys, WIDTH), BF16),
            pltpu.VMEM((WIDTH, keys), BF16),
            pltpu.VMEM((keys, BLOCK), F32),
            pltpu.VMEM((2 * keys, cols), F32),
            pltpu.VMEM((2 * keys, cols), F32),
            pltpu.VMEM((2 * keys, cols), F32),
            pltpu.VMEM((WIDTH, HEADS * BLOCK), F32),
            pltpu.VMEM((keys, 2 * WIDTH), F32),
            pltpu.SMEM((1,), jnp.int32),
            pltpu.SMEM((KEY_BLOCKS + 1,), jnp.int32),
        ],
        compiler_params=pltpu.CompilerParams(vmem_limit_bytes=56 * 1024 * 1024),
    )(order, stripes, q, do, *kvs)


FIXED = 16
OTHERS = tuple(m for m in range(1, 32) if m != FIXED)


def plan_kernel(partner_ref, k_ref, v_ref, first_ref, second_ref, third_ref, order_ref, payload_ref):
    payload_ref[:, :WIDTH] = k_ref[...]
    payload_ref[:, WIDTH:] = v_ref[...]
    masks = [partner_ref[r, 0] for r in range(ROUNDS)]
    rest = [jnp.where(masks[r] == FIXED, masks[ROUNDS - 1], masks[r]) for r in range(ROUNDS - 1)]
    for ref, mask in zip((first_ref, second_ref, third_ref), rest):
        ref[0] = jnp.where(mask > FIXED, mask - 2, mask - 1)
    for r, mask in enumerate((0, FIXED, *rest)):
        order_ref[r] = mask


def plan(partner, key_rows, value_rows):
    vmem, smem = pl.BlockSpec(memory_space=pltpu.VMEM), pl.BlockSpec(memory_space=pltpu.SMEM)
    one = jax.ShapeDtypeStruct((1,), jnp.int32)
    return pl.pallas_call(
        plan_kernel,
        out_shape=[one, one, one, jax.ShapeDtypeStruct((ROUNDS + 1,), jnp.int32), jax.ShapeDtypeStruct((ROWS, 2 * WIDTH), BF16)],
        in_specs=[smem, vmem, vmem],
        out_specs=[smem] * 4 + [vmem],
    )(partner.T, key_rows, value_rows)


def finish_kernel(own, p1, p2, p3, p4, dk_ref, dv_ref):
    for ref, cols in ((dk_ref, slice(0, WIDTH)), (dv_ref, slice(WIDTH, 2 * WIDTH))):
        acc = own[:, cols]
        for p in (p1, p2, p3, p4):
            acc += p[:, cols].astype(F32)
        ref[...] = acc.astype(BF16)


def finish(own, parts):
    return pl.pallas_call(finish_kernel, out_shape=[jax.ShapeDtypeStruct((ROWS, WIDTH), BF16)] * 2)(own, *parts)


def swap_kernel(mask, mine, theirs, sent, came):
    partner = {"ctx": lax.axis_index("ctx") ^ mask}
    entered = pltpu.get_barrier_semaphore()
    pl.semaphore_signal(entered, inc=1, device_id=partner, device_id_type=MESH)
    pl.semaphore_wait(entered, 1)
    copy = pltpu.make_async_remote_copy(
        src_ref=mine, dst_ref=theirs, send_sem=sent, recv_sem=came, device_id=partner, device_id_type=MESH
    )
    copy.start()
    copy.wait()


def swap(mask, number, x):
    spec = pl.BlockSpec(memory_space=pl.ANY)
    return pl.pallas_call(
        functools.partial(swap_kernel, mask),
        out_shape=jax.ShapeDtypeStruct(x.shape, x.dtype),
        in_specs=[spec],
        out_specs=spec,
        scratch_shapes=[pltpu.SemaphoreType.DMA, pltpu.SemaphoreType.DMA],
        compiler_params=pltpu.CompilerParams(collective_id=number, has_side_effects=True),
    )(x)


def exchange(branch, arrays):
    fixed, *rest = arrays
    by = [functools.partial(swap, m, i) for i, m in enumerate(OTHERS)]
    across = lax.ppermute(fixed, "ctx", [(i, i ^ FIXED) for i in range(32)])
    return [across, *(lax.switch(b, by, x) for b, x in zip(branch, rest))]


def local(queries, key_rows, value_rows, out_grad, partner, stripes):
    *branch, order, payload = plan(partner, key_rows, value_rows)
    branch = [b.reshape(()) for b in branch]
    kvs = exchange(branch, (payload,) * ROUNDS)
    dq, own, *parts = attend(order, stripes, queries, out_grad, (payload, *kvs))
    return (dq, *finish(own, exchange(branch, parts)))


def solution(mesh):
    return jax.shard_map(
        local,
        mesh=mesh,
        in_specs=(P("ctx", "head"), P("ctx", "head"), P("ctx", "head"), P("ctx", "head"), P(), P()),
        out_specs=(P("ctx", "head"), P("ctx", "head"), P("ctx", "head")),
        check_vma=False,
    )
```

```python
import functools
import math

import jax
import jax.numpy as jnp
from jax import lax
from jax.experimental import pallas as pl
from jax.experimental.pallas import tpu as pltpu
from jax.sharding import PartitionSpec as P

HEADS = 16
SPLIT = 4
WIDTH = 128
BLOCK = 128
OWNED = 3
ROUNDS = 4
ROWS = OWNED * BLOCK
KEY_BLOCKS = OWNED * (ROUNDS + 1)
SCALE = 1.0 / math.sqrt(WIDTH)
SCALE_LOG2 = SCALE * math.log2(math.e)
MESH = pl.DeviceIdType.MESH
F32 = jnp.float32
BF16 = jnp.bfloat16
NT = (((1,), (1,)), ((), ()))


def attend_kernel(
    order_ref, stripes_ref, q_ref, do_ref, kv0, kv1, kv2, kv3, kv4,
    dq_ref, g0, g1, g2, g3, g4,
    kc, vc, kt, bias, m_scr, dp_scr, p_scr, dqt, qs, dos, total, count, order,
):
    kvs = (kv0, kv1, kv2, kv3, kv4)
    grads = (g0, g1, g2, g3, g4)
    a = pl.program_id(0)
    device = lax.axis_index("ctx")

    def place_of(j):
        return stripes_ref[(device ^ order_ref[j // OWNED]) * OWNED + j % OWNED]

    @pl.when(a == 0)
    def _():
        total[...] = jnp.zeros_like(total)
        bias[...] = jnp.zeros_like(bias)
        key = lax.broadcasted_iota(jnp.int32, (BLOCK, BLOCK), 0)
        query = lax.broadcasted_iota(jnp.int32, (BLOCK, BLOCK), 1)
        bias[:BLOCK, :] = jnp.where(key <= query, 0.0, -1e30)

    def block(i):
        return pl.ds(pl.multiple_of(i * BLOCK, BLOCK), BLOCK)

    def put(ref, start, slot):
        src = pl.ds(start, BLOCK)
        k = ref[src, :WIDTH]
        kc[block(slot), :] = k
        vc[block(slot), :] = ref[src, WIDTH:]
        kt[:, block(slot)] = k.T

    place = stripes_ref[device * OWNED + a]
    put(kv0, pl.multiple_of(a * BLOCK, BLOCK), 0)
    order[0] = a
    count[0] = 1
    for j in range(KEY_BLOCKS):
        @pl.when(place_of(j) < place)
        def _():
            slot = count[0]
            put(kvs[j // OWNED], (j % OWNED) * BLOCK, slot)
            order[slot] = j
            count[0] = slot + 1
    n = count[0]
    odd = lax.rem(n, 2) == 1
    chunks = (n + 1) // 2

    @pl.when(odd)
    def _():
        kc[block(n), :] = jnp.zeros((BLOCK, WIDTH), BF16)
        vc[block(n), :] = jnp.zeros((BLOCK, WIDTH), BF16)
        kt[:, block(n)] = jnp.zeros((WIDTH, BLOCK), BF16)
        bias[block(n), :] = jnp.full((BLOCK, BLOCK), -1e30, F32)
        order[n] = KEY_BLOCKS

    for h in range(HEADS):
        qs[h * BLOCK : (h + 1) * BLOCK, :] = q_ref[:, h * WIDTH : (h + 1) * WIDTH]
        dos[h * BLOCK : (h + 1) * BLOCK, :] = do_ref[:, h * WIDTH : (h + 1) * WIDTH]

    span = HEADS * BLOCK // SPLIT
    spans = [slice(i * span, (i + 1) * span) for i in range(SPLIT)]

    def fold(x, op):
        return op(x.reshape(x.shape[0] // 8, 8, x.shape[1]), axis=0)

    def chunk_rows(c):
        return pl.ds(pl.multiple_of(c * 256, 256), 256), pl.ds(pl.multiple_of(c * 8, 8), 8)

    def probabilities(c, carry):
        high, norm, weighted = (list(x) for x in carry)
        rows, state = chunk_rows(c)
        mask = bias[rows, :]
        for i, at in enumerate(spans):
            s = lax.dot_general(kc[rows, :], qs[at, :], NT, preferred_element_type=F32)
            s += jnp.concatenate([mask] * (span // BLOCK), axis=1)
            new = jnp.maximum(high[i], jnp.max(fold(s, jnp.max), axis=0, keepdims=True))
            p = jnp.exp2((s - new) * SCALE_LOG2)
            dp = lax.dot_general(vc[rows, :], dos[at, :], NT, preferred_element_type=F32)
            shrink = jnp.exp2((high[i] - new) * SCALE_LOG2)
            norm[i] = norm[i] * shrink + fold(p, jnp.sum)
            weighted[i] = weighted[i] * shrink + fold(p * dp, jnp.sum)
            high[i] = new
            m_scr[state, at] = jnp.broadcast_to(new, (8, span))
            p_scr[rows, at] = p
            dp_scr[rows, at] = dp
        return tuple(high), tuple(norm), tuple(weighted)

    zero = (jnp.zeros((8, span), F32),) * SPLIT
    low = (jnp.full((1, span), -1e30, F32),) * SPLIT
    high, norm, weighted = lax.fori_loop(0, chunks, probabilities, (low, zero, zero))
    inverse = [1.0 / jnp.sum(x, axis=0, keepdims=True) for x in norm]
    delta = [jnp.sum(x, axis=0, keepdims=True) * y for x, y in zip(weighted, inverse)]
    dqt[...] = jnp.zeros_like(dqt)

    def products(c, _):
        rows, state = chunk_rows(c)
        dk = dv = None
        for i, at in enumerate(spans):
            factor = jnp.exp2((m_scr[state, at][:1] - high[i]) * SCALE_LOG2) * inverse[i]
            p = p_scr[rows, at] * factor
            ds = (p * (dp_scr[rows, at] - delta[i])).astype(BF16)
            dk_part = jnp.dot(ds, qs[at, :], preferred_element_type=F32)
            dv_part = jnp.dot(p.astype(BF16), dos[at, :], preferred_element_type=F32)
            dk, dv = (dk_part, dv_part) if dk is None else (dk + dk_part, dv + dv_part)
            dqt[:, at] += jnp.dot(kt[:, rows], ds, preferred_element_type=F32)
        for half in range(2):
            here, part = block(order[2 * c + half]), slice(half * BLOCK, half * BLOCK + BLOCK)
            total[here, :WIDTH] += dk[part]
            total[here, WIDTH:] += dv[part]
        return 0

    lax.fori_loop(0, chunks, products, 0)
    for h in range(HEADS):
        here = slice(h * WIDTH, h * WIDTH + WIDTH)
        dq_ref[:, here] = (dqt[:, here] * SCALE).astype(BF16).T

    @pl.when(odd)
    def _():
        bias[block(n), :] = jnp.zeros((BLOCK, BLOCK), F32)

    @pl.when(a == OWNED - 1)
    def _():
        for s in range(ROUNDS + 1):
            rows = slice(s * ROWS, (s + 1) * ROWS)
            grads[s][:, :WIDTH] = (total[rows, :WIDTH] * SCALE).astype(grads[s].dtype)
            grads[s][:, WIDTH:] = total[rows, WIDTH:].astype(grads[s].dtype)


def attend(order, stripes, q, do, kvs):
    smem = pl.BlockSpec(memory_space=pltpu.SMEM)
    part = pl.BlockSpec((ROWS, 2 * WIDTH), lambda a: (0, 0))
    rows = pl.BlockSpec((BLOCK, HEADS * WIDTH), lambda a: (a, 0))
    keys = (KEY_BLOCKS + 1) * BLOCK
    cols = HEADS * BLOCK
    return pl.pallas_call(
        attend_kernel,
        out_shape=[jax.ShapeDtypeStruct(q.shape, BF16), jax.ShapeDtypeStruct((ROWS, 2 * WIDTH), F32)]
        + [jax.ShapeDtypeStruct((ROWS, 2 * WIDTH), BF16)] * ROUNDS,
        grid=(OWNED,),
        in_specs=[smem, smem, rows, rows] + [part] * (ROUNDS + 1),
        out_specs=[rows] + [part] * (ROUNDS + 1),
        scratch_shapes=[
            pltpu.VMEM((keys, WIDTH), BF16),
            pltpu.VMEM((keys, WIDTH), BF16),
            pltpu.VMEM((WIDTH, keys), BF16),
            pltpu.VMEM((keys, BLOCK), F32),
            pltpu.VMEM(((KEY_BLOCKS + 1) // 2 * 8, cols), F32),
            pltpu.VMEM((keys, cols), F32),
            pltpu.VMEM((keys, cols), F32),
            pltpu.VMEM((WIDTH, HEADS * BLOCK), F32),
            pltpu.VMEM((HEADS * BLOCK, WIDTH), BF16),
            pltpu.VMEM((HEADS * BLOCK, WIDTH), BF16),
            pltpu.VMEM((keys, 2 * WIDTH), F32),
            pltpu.SMEM((1,), jnp.int32),
            pltpu.SMEM((KEY_BLOCKS + 1,), jnp.int32),
        ],
        compiler_params=pltpu.CompilerParams(vmem_limit_bytes=56 * 1024 * 1024),
    )(order, stripes, q, do, *kvs)


FIXED = 16
OTHERS = tuple(m for m in range(1, 32) if m != FIXED)


def plan_kernel(partner_ref, k_ref, v_ref, first_ref, second_ref, third_ref, order_ref, payload_ref):
    payload_ref[:, :WIDTH] = k_ref[...]
    payload_ref[:, WIDTH:] = v_ref[...]
    masks = [partner_ref[r, 0] for r in range(ROUNDS)]
    rest = [jnp.where(masks[r] == FIXED, masks[ROUNDS - 1], masks[r]) for r in range(ROUNDS - 1)]
    for ref, mask in zip((first_ref, second_ref, third_ref), rest):
        ref[0] = jnp.where(mask > FIXED, mask - 2, mask - 1)
    for r, mask in enumerate((0, FIXED, *rest)):
        order_ref[r] = mask


def plan(partner, key_rows, value_rows):
    vmem, smem = pl.BlockSpec(memory_space=pltpu.VMEM), pl.BlockSpec(memory_space=pltpu.SMEM)
    one = jax.ShapeDtypeStruct((1,), jnp.int32)
    return pl.pallas_call(
        plan_kernel,
        out_shape=[one, one, one, jax.ShapeDtypeStruct((ROUNDS + 1,), jnp.int32), jax.ShapeDtypeStruct((ROWS, 2 * WIDTH), BF16)],
        in_specs=[smem, vmem, vmem],
        out_specs=[smem] * 4 + [vmem],
    )(partner.T, key_rows, value_rows)


def finish_kernel(own, p1, p2, p3, p4, dk_ref, dv_ref):
    for ref, cols in ((dk_ref, slice(0, WIDTH)), (dv_ref, slice(WIDTH, 2 * WIDTH))):
        acc = own[:, cols]
        for p in (p1, p2, p3, p4):
            acc += p[:, cols].astype(F32)
        ref[...] = acc.astype(BF16)


def finish(own, parts):
    return pl.pallas_call(finish_kernel, out_shape=[jax.ShapeDtypeStruct((ROWS, WIDTH), BF16)] * 2)(own, *parts)


def swap_kernel(mask, mine, theirs, sent, came):
    partner = {"ctx": lax.axis_index("ctx") ^ mask}
    entered = pltpu.get_barrier_semaphore()
    pl.semaphore_signal(entered, inc=1, device_id=partner, device_id_type=MESH)
    pl.semaphore_wait(entered, 1)
    copy = pltpu.make_async_remote_copy(
        src_ref=mine, dst_ref=theirs, send_sem=sent, recv_sem=came, device_id=partner, device_id_type=MESH
    )
    copy.start()
    copy.wait()


def swap(mask, number, x):
    spec = pl.BlockSpec(memory_space=pl.ANY)
    return pl.pallas_call(
        functools.partial(swap_kernel, mask),
        out_shape=jax.ShapeDtypeStruct(x.shape, x.dtype),
        in_specs=[spec],
        out_specs=spec,
        scratch_shapes=[pltpu.SemaphoreType.DMA, pltpu.SemaphoreType.DMA],
        compiler_params=pltpu.CompilerParams(collective_id=number, has_side_effects=True),
    )(x)


def exchange(branch, arrays):
    fixed, *rest = arrays
    by = [functools.partial(swap, m, i) for i, m in enumerate(OTHERS)]
    across = lax.ppermute(fixed, "ctx", [(i, i ^ FIXED) for i in range(32)])
    return [across, *(lax.switch(b, by, x) for b, x in zip(branch, rest))]


def local(queries, key_rows, value_rows, out_grad, partner, stripes):
    *branch, order, payload = plan(partner, key_rows, value_rows)
    branch = [b.reshape(()) for b in branch]
    kvs = exchange(branch, (payload,) * ROUNDS)
    dq, own, *parts = attend(order, stripes, queries, out_grad, (payload, *kvs))
    return (dq, *finish(own, exchange(branch, parts)))


def solution(mesh):
    return jax.shard_map(
        local,
        mesh=mesh,
        in_specs=(P("ctx", "head"), P("ctx", "head"), P("ctx", "head"), P("ctx", "head"), P(), P()),
        out_specs=(P("ctx", "head"), P("ctx", "head"), P("ctx", "head")),
        check_vma=False,
    )
```

```python
import functools
import math

import jax
import jax.numpy as jnp
from jax import lax
from jax.experimental import pallas as pl
from jax.experimental.pallas import tpu as pltpu
from jax.sharding import PartitionSpec as P

HEADS = 16
SPLIT_A = 1
SPLIT_B = 8
WIDTH = 128
BLOCK = 128
PAIR = 2 * BLOCK
OWNED = 3
ROUNDS = 4
ROWS = OWNED * BLOCK
KEY_BLOCKS = OWNED * (ROUNDS + 1)
SCALE = 1.0 / math.sqrt(WIDTH)
SCALE_LOG2 = SCALE * math.log2(math.e)
MESH = pl.DeviceIdType.MESH
F32 = jnp.float32
BF16 = jnp.bfloat16
NT = (((1,), (1,)), ((), ()))


def attend_kernel(
    order_ref, stripes_ref, q_ref, do_ref, kv0, kv1, kv2, kv3, kv4,
    dq_ref, g0, g1, g2, g3, g4,
    kc, vc, kt, bias, m_scr, dp_scr, p_scr, dqt, qs, dos, total, count, order,
):
    kvs = (kv0, kv1, kv2, kv3, kv4)
    grads = (g0, g1, g2, g3, g4)
    a = pl.program_id(0)
    device = lax.axis_index("ctx")

    def place_of(j):
        return stripes_ref[(device ^ order_ref[j // OWNED]) * OWNED + j % OWNED]

    @pl.when(a == 0)
    def _():
        total[...] = jnp.zeros_like(total)
        bias[...] = jnp.zeros_like(bias)
        key = lax.broadcasted_iota(jnp.int32, (BLOCK, BLOCK), 0)
        query = lax.broadcasted_iota(jnp.int32, (BLOCK, BLOCK), 1)
        bias[:BLOCK, :] = jnp.where(key <= query, 0.0, -1e30)

    def block(i):
        return pl.ds(pl.multiple_of(i * BLOCK, BLOCK), BLOCK)

    def put(ref, start, slot):
        src = pl.ds(start, BLOCK)
        k = ref[src, :WIDTH]
        kc[block(slot), :] = k
        vc[block(slot), :] = ref[src, WIDTH:]
        kt[:, block(slot)] = k.T

    place = stripes_ref[device * OWNED + a]
    put(kv0, pl.multiple_of(a * BLOCK, BLOCK), 0)
    order[0] = a
    count[0] = 1
    for j in range(KEY_BLOCKS):
        @pl.when(place_of(j) < place)
        def _():
            slot = count[0]
            put(kvs[j // OWNED], (j % OWNED) * BLOCK, slot)
            order[slot] = j
            count[0] = slot + 1
    n = count[0]
    full, odd = n // 2, lax.rem(n, 2)

    for h in range(HEADS):
        qs[h * BLOCK : (h + 1) * BLOCK, :] = q_ref[:, h * WIDTH : (h + 1) * WIDTH]
        dos[h * BLOCK : (h + 1) * BLOCK, :] = do_ref[:, h * WIDTH : (h + 1) * WIDTH]

    def spans(count):
        width = HEADS * BLOCK // count
        return [slice(i * width, (i + 1) * width) for i in range(count)]

    def fold(x, op):
        return op(x.reshape(x.shape[0] // 8, 8, x.shape[1]), axis=0)

    def chunk_rows(c, size):
        return pl.ds(pl.multiple_of(c * PAIR, PAIR), size), pl.ds(pl.multiple_of(c * 8, 8), 8)

    def probabilities(c, carry, size=PAIR, masked=True):
        high, norm, weighted = (list(x) for x in carry)
        rows, state = chunk_rows(c, size)
        for i, at in enumerate(spans(SPLIT_A)):
            s = lax.dot_general(kc[rows, :], qs[at, :], NT, preferred_element_type=F32)
            if masked:
                s += jnp.concatenate([bias[rows, :]] * (span // BLOCK), axis=1)
            new = jnp.maximum(high[i], jnp.max(fold(s, jnp.max), axis=0, keepdims=True))
            p = jnp.exp2((s - new) * SCALE_LOG2)
            dp = lax.dot_general(vc[rows, :], dos[at, :], NT, preferred_element_type=F32)
            shrink = jnp.exp2((high[i] - new) * SCALE_LOG2)
            norm[i] = norm[i] * shrink + fold(p, jnp.sum)
            weighted[i] = weighted[i] * shrink + fold(p * dp, jnp.sum)
            high[i] = new
            m_scr[state, at] = jnp.broadcast_to(new, (8, span))
            p_scr[rows, at] = p
            dp_scr[rows, at] = dp
        return tuple(high), tuple(norm), tuple(weighted)

    span = HEADS * BLOCK // SPLIT_A
    zero = (jnp.zeros((8, span), F32),) * SPLIT_A
    low = (jnp.full((1, span), -1e30, F32),) * SPLIT_A
    stats = lax.fori_loop(0, jnp.minimum(full, 1), probabilities, (low, zero, zero))
    stats = lax.fori_loop(1, full, functools.partial(probabilities, masked=False), stats)
    high, norm, weighted = lax.fori_loop(full, full + odd, functools.partial(probabilities, size=BLOCK), stats)
    high, norm, weighted = (jnp.concatenate(x, axis=1) for x in (high, norm, weighted))
    inverse = 1.0 / jnp.sum(norm, axis=0, keepdims=True)
    delta = jnp.sum(weighted, axis=0, keepdims=True) * inverse
    dqt[...] = jnp.zeros_like(dqt)

    def products(c, _, size=PAIR):
        rows, state = chunk_rows(c, size)
        dk = dv = None
        for i, at in enumerate(spans(SPLIT_B)):
            factor = jnp.exp2((m_scr[state, at][:1] - high[:, at]) * SCALE_LOG2) * inverse[:, at]
            p = p_scr[rows, at] * factor
            ds = (p * (dp_scr[rows, at] - delta[:, at])).astype(BF16)
            dk_part = jnp.dot(ds, qs[at, :], preferred_element_type=F32)
            dv_part = jnp.dot(p.astype(BF16), dos[at, :], preferred_element_type=F32)
            dk, dv = (dk_part, dv_part) if dk is None else (dk + dk_part, dv + dv_part)
            dqt[:, at] += jnp.dot(kt[:, rows], ds, preferred_element_type=F32)
        for half in range(size // BLOCK):
            here, part = block(order[2 * c + half]), slice(half * BLOCK, half * BLOCK + BLOCK)
            total[here, :WIDTH] += dk[part]
            total[here, WIDTH:] += dv[part]
        return 0

    lax.fori_loop(0, full, products, 0)
    lax.fori_loop(full, full + odd, functools.partial(products, size=BLOCK), 0)
    for h in range(HEADS):
        here = slice(h * WIDTH, h * WIDTH + WIDTH)
        dq_ref[:, here] = (dqt[:, here] * SCALE).astype(BF16).T

    @pl.when(a == OWNED - 1)
    def _():
        for s in range(ROUNDS + 1):
            rows = slice(s * ROWS, (s + 1) * ROWS)
            grads[s][:, :WIDTH] = (total[rows, :WIDTH] * SCALE).astype(grads[s].dtype)
            grads[s][:, WIDTH:] = total[rows, WIDTH:].astype(grads[s].dtype)


def attend(order, stripes, q, do, kvs):
    smem = pl.BlockSpec(memory_space=pltpu.SMEM)
    part = pl.BlockSpec((ROWS, 2 * WIDTH), lambda a: (0, 0))
    rows = pl.BlockSpec((BLOCK, HEADS * WIDTH), lambda a: (a, 0))
    keys = (KEY_BLOCKS + 1) * BLOCK
    cols = HEADS * BLOCK
    return pl.pallas_call(
        attend_kernel,
        out_shape=[jax.ShapeDtypeStruct(q.shape, BF16), jax.ShapeDtypeStruct((ROWS, 2 * WIDTH), F32)]
        + [jax.ShapeDtypeStruct((ROWS, 2 * WIDTH), BF16)] * ROUNDS,
        grid=(OWNED,),
        in_specs=[smem, smem, rows, rows] + [part] * (ROUNDS + 1),
        out_specs=[rows] + [part] * (ROUNDS + 1),
        scratch_shapes=[
            pltpu.VMEM((keys, WIDTH), BF16),
            pltpu.VMEM((keys, WIDTH), BF16),
            pltpu.VMEM((WIDTH, keys), BF16),
            pltpu.VMEM((keys, BLOCK), F32),
            pltpu.VMEM(((KEY_BLOCKS + 1) // 2 * 8, cols), F32),
            pltpu.VMEM((keys, cols), F32),
            pltpu.VMEM((keys, cols), F32),
            pltpu.VMEM((WIDTH, HEADS * BLOCK), F32),
            pltpu.VMEM((HEADS * BLOCK, WIDTH), BF16),
            pltpu.VMEM((HEADS * BLOCK, WIDTH), BF16),
            pltpu.VMEM((keys, 2 * WIDTH), F32),
            pltpu.SMEM((1,), jnp.int32),
            pltpu.SMEM((KEY_BLOCKS + 1,), jnp.int32),
        ],
        compiler_params=pltpu.CompilerParams(vmem_limit_bytes=56 * 1024 * 1024),
    )(order, stripes, q, do, *kvs)


FIXED = 16
OTHERS = tuple(m for m in range(1, 32) if m != FIXED)


def plan_kernel(partner_ref, k_ref, v_ref, first_ref, second_ref, third_ref, order_ref, payload_ref):
    payload_ref[:, :WIDTH] = k_ref[...]
    payload_ref[:, WIDTH:] = v_ref[...]
    masks = [partner_ref[r, 0] for r in range(ROUNDS)]
    rest = [jnp.where(masks[r] == FIXED, masks[ROUNDS - 1], masks[r]) for r in range(ROUNDS - 1)]
    for ref, mask in zip((first_ref, second_ref, third_ref), rest):
        ref[0] = jnp.where(mask > FIXED, mask - 2, mask - 1)
    for r, mask in enumerate((0, FIXED, *rest)):
        order_ref[r] = mask


def plan(partner, key_rows, value_rows):
    vmem, smem = pl.BlockSpec(memory_space=pltpu.VMEM), pl.BlockSpec(memory_space=pltpu.SMEM)
    one = jax.ShapeDtypeStruct((1,), jnp.int32)
    return pl.pallas_call(
        plan_kernel,
        out_shape=[one, one, one, jax.ShapeDtypeStruct((ROUNDS + 1,), jnp.int32), jax.ShapeDtypeStruct((ROWS, 2 * WIDTH), BF16)],
        in_specs=[smem, vmem, vmem],
        out_specs=[smem] * 4 + [vmem],
    )(partner.T, key_rows, value_rows)


def finish_kernel(own, p1, p2, p3, p4, dk_ref, dv_ref):
    for ref, cols in ((dk_ref, slice(0, WIDTH)), (dv_ref, slice(WIDTH, 2 * WIDTH))):
        acc = own[:, cols]
        for p in (p1, p2, p3, p4):
            acc += p[:, cols].astype(F32)
        ref[...] = acc.astype(BF16)


def finish(own, parts):
    return pl.pallas_call(finish_kernel, out_shape=[jax.ShapeDtypeStruct((ROWS, WIDTH), BF16)] * 2)(own, *parts)


def swap_kernel(mask, mine, theirs, sent, came):
    partner = {"ctx": lax.axis_index("ctx") ^ mask}
    entered = pltpu.get_barrier_semaphore()
    pl.semaphore_signal(entered, inc=1, device_id=partner, device_id_type=MESH)
    pl.semaphore_wait(entered, 1)
    copy = pltpu.make_async_remote_copy(
        src_ref=mine, dst_ref=theirs, send_sem=sent, recv_sem=came, device_id=partner, device_id_type=MESH
    )
    copy.start()
    copy.wait()


def swap(mask, number, x):
    spec = pl.BlockSpec(memory_space=pl.ANY)
    return pl.pallas_call(
        functools.partial(swap_kernel, mask),
        out_shape=jax.ShapeDtypeStruct(x.shape, x.dtype),
        in_specs=[spec],
        out_specs=spec,
        scratch_shapes=[pltpu.SemaphoreType.DMA, pltpu.SemaphoreType.DMA],
        compiler_params=pltpu.CompilerParams(collective_id=number, has_side_effects=True),
    )(x)


def exchange(branch, arrays):
    fixed, *rest = arrays
    by = [functools.partial(swap, m, i) for i, m in enumerate(OTHERS)]
    across = lax.ppermute(fixed, "ctx", [(i, i ^ FIXED) for i in range(32)])
    return [across, *(lax.switch(b, by, x) for b, x in zip(branch, rest))]


def local(queries, key_rows, value_rows, out_grad, partner, stripes):
    *branch, order, payload = plan(partner, key_rows, value_rows)
    branch = [b.reshape(()) for b in branch]
    kvs = exchange(branch, (payload,) * ROUNDS)
    dq, own, *parts = attend(order, stripes, queries, out_grad, (payload, *kvs))
    return (dq, *finish(own, exchange(branch, parts)))


def solution(mesh):
    return jax.shard_map(
        local,
        mesh=mesh,
        in_specs=(P("ctx", "head"), P("ctx", "head"), P("ctx", "head"), P("ctx", "head"), P(), P()),
        out_specs=(P("ctx", "head"), P("ctx", "head"), P("ctx", "head")),
        check_vma=False,
    )
```

```python
import functools
import math

import jax
import jax.numpy as jnp
from jax import lax
from jax.experimental import pallas as pl
from jax.experimental.pallas import tpu as pltpu
from jax.sharding import PartitionSpec as P

HEADS = 16
SPLIT_A = 1
SPLIT_B = 8
WIDTH = 128
BLOCK = 128
PAIR = 2 * BLOCK
OWNED = 3
ROUNDS = 4
ROWS = OWNED * BLOCK
KEY_BLOCKS = OWNED * (ROUNDS + 1)
SCALE = 1.0 / math.sqrt(WIDTH)
SCALE_LOG2 = SCALE * math.log2(math.e)
MESH = pl.DeviceIdType.MESH
F32 = jnp.float32
BF16 = jnp.bfloat16
NT = (((1,), (1,)), ((), ()))


def attend_kernel(
    order_ref, stripes_ref, q_ref, do_ref, kv0, kv1, kv2, kv3, kv4,
    dq_ref, g0, g1, g2, g3, g4,
    kc, vc, kt, bias, m_scr, dp_scr, p_scr, dqt, qs, dos, kt_all, total, count, order,
):
    kvs = (kv0, kv1, kv2, kv3, kv4)
    grads = (g0, g1, g2, g3, g4)
    a = pl.program_id(0)
    device = lax.axis_index("ctx")

    def place_of(j):
        return stripes_ref[(device ^ order_ref[j // OWNED]) * OWNED + j % OWNED]

    @pl.when(a == 0)
    def _():
        total[...] = jnp.zeros_like(total)
        bias[...] = jnp.zeros_like(bias)
        key = lax.broadcasted_iota(jnp.int32, (BLOCK, BLOCK), 0)
        query = lax.broadcasted_iota(jnp.int32, (BLOCK, BLOCK), 1)
        bias[:BLOCK, :] = jnp.where(key <= query, 0.0, -1e30)
        for j in range(KEY_BLOCKS):
            at = j % OWNED * BLOCK
            kt_all[:, j * BLOCK : (j + 1) * BLOCK] = kvs[j // OWNED][at : at + BLOCK, :WIDTH].T

    def block(i):
        return pl.ds(pl.multiple_of(i * BLOCK, BLOCK), BLOCK)

    def put(ref, start, slot, j):
        src = pl.ds(start, BLOCK)
        kc[block(slot), :] = ref[src, :WIDTH]
        vc[block(slot), :] = ref[src, WIDTH:]
        kt[:, block(slot)] = kt_all[:, block(j)]

    place = stripes_ref[device * OWNED + a]
    put(kv0, pl.multiple_of(a * BLOCK, BLOCK), 0, a)
    order[0] = a
    count[0] = 1
    for j in range(KEY_BLOCKS):
        @pl.when(place_of(j) < place)
        def _():
            slot = count[0]
            put(kvs[j // OWNED], (j % OWNED) * BLOCK, slot, j)
            order[slot] = j
            count[0] = slot + 1
    n = count[0]
    full, odd = n // 2, lax.rem(n, 2)

    for h in range(HEADS):
        qs[h * BLOCK : (h + 1) * BLOCK, :] = q_ref[:, h * WIDTH : (h + 1) * WIDTH]
        dos[h * BLOCK : (h + 1) * BLOCK, :] = do_ref[:, h * WIDTH : (h + 1) * WIDTH]

    def spans(count):
        width = HEADS * BLOCK // count
        return [slice(i * width, (i + 1) * width) for i in range(count)]

    def fold(x, op):
        return op(x.reshape(x.shape[0] // 8, 8, x.shape[1]), axis=0)

    def chunk_rows(c, size):
        return pl.ds(pl.multiple_of(c * PAIR, PAIR), size), pl.ds(pl.multiple_of(c * 8, 8), 8)

    def probabilities(c, carry, size=PAIR, masked=True):
        high, norm, weighted = (list(x) for x in carry)
        rows, state = chunk_rows(c, size)
        for i, at in enumerate(spans(SPLIT_A)):
            s = lax.dot_general(kc[rows, :], qs[at, :], NT, preferred_element_type=F32)
            if masked:
                s += jnp.concatenate([bias[rows, :]] * (span // BLOCK), axis=1)
            new = jnp.maximum(high[i], jnp.max(fold(s, jnp.max), axis=0, keepdims=True))
            p = jnp.exp2((s - new) * SCALE_LOG2)
            dp = lax.dot_general(vc[rows, :], dos[at, :], NT, preferred_element_type=F32)
            shrink = jnp.exp2((high[i] - new) * SCALE_LOG2)
            norm[i] = norm[i] * shrink + fold(p, jnp.sum)
            weighted[i] = weighted[i] * shrink + fold(p * dp, jnp.sum)
            high[i] = new
            m_scr[state, at] = jnp.broadcast_to(new, (8, span))
            p_scr[rows, at] = p
            dp_scr[rows, at] = dp
        return tuple(high), tuple(norm), tuple(weighted)

    span = HEADS * BLOCK // SPLIT_A
    zero = (jnp.zeros((8, span), F32),) * SPLIT_A
    low = (jnp.full((1, span), -1e30, F32),) * SPLIT_A
    stats = lax.fori_loop(0, jnp.minimum(full, 1), probabilities, (low, zero, zero))
    stats = lax.fori_loop(1, full, functools.partial(probabilities, masked=False), stats)
    high, norm, weighted = lax.fori_loop(full, full + odd, functools.partial(probabilities, size=BLOCK), stats)
    high, norm, weighted = (jnp.concatenate(x, axis=1) for x in (high, norm, weighted))
    inverse = 1.0 / jnp.sum(norm, axis=0, keepdims=True)
    delta = jnp.sum(weighted, axis=0, keepdims=True) * inverse
    dqt[...] = jnp.zeros_like(dqt)

    def products(c, _, size=PAIR):
        rows, state = chunk_rows(c, size)
        dk = dv = None
        for i, at in enumerate(spans(SPLIT_B)):
            factor = jnp.exp2((m_scr[state, at][:1] - high[:, at]) * SCALE_LOG2) * inverse[:, at]
            p = p_scr[rows, at] * factor
            ds = (p * (dp_scr[rows, at] - delta[:, at])).astype(BF16)
            dk_part = jnp.dot(ds, qs[at, :], preferred_element_type=F32)
            dv_part = jnp.dot(p.astype(BF16), dos[at, :], preferred_element_type=F32)
            dk, dv = (dk_part, dv_part) if dk is None else (dk + dk_part, dv + dv_part)
            dqt[:, at] += jnp.dot(kt[:, rows], ds, preferred_element_type=F32)
        for half in range(size // BLOCK):
            here, part = block(order[2 * c + half]), slice(half * BLOCK, half * BLOCK + BLOCK)
            total[here, :WIDTH] += dk[part]
            total[here, WIDTH:] += dv[part]
        return 0

    lax.fori_loop(0, full, products, 0)
    lax.fori_loop(full, full + odd, functools.partial(products, size=BLOCK), 0)
    for h in range(HEADS):
        here = slice(h * WIDTH, h * WIDTH + WIDTH)
        dq_ref[:, here] = (dqt[:, here] * SCALE).astype(BF16).T

    @pl.when(a == OWNED - 1)
    def _():
        for s in range(ROUNDS + 1):
            rows = slice(s * ROWS, (s + 1) * ROWS)
            grads[s][:, :WIDTH] = (total[rows, :WIDTH] * SCALE).astype(grads[s].dtype)
            grads[s][:, WIDTH:] = total[rows, WIDTH:].astype(grads[s].dtype)


def attend(order, stripes, q, do, kvs):
    smem = pl.BlockSpec(memory_space=pltpu.SMEM)
    part = pl.BlockSpec((ROWS, 2 * WIDTH), lambda a: (0, 0))
    rows = pl.BlockSpec((BLOCK, HEADS * WIDTH), lambda a: (a, 0))
    keys = (KEY_BLOCKS + 1) * BLOCK
    cols = HEADS * BLOCK
    return pl.pallas_call(
        attend_kernel,
        out_shape=[jax.ShapeDtypeStruct(q.shape, BF16), jax.ShapeDtypeStruct((ROWS, 2 * WIDTH), F32)]
        + [jax.ShapeDtypeStruct((ROWS, 2 * WIDTH), BF16)] * ROUNDS,
        grid=(OWNED,),
        in_specs=[smem, smem, rows, rows] + [part] * (ROUNDS + 1),
        out_specs=[rows] + [part] * (ROUNDS + 1),
        scratch_shapes=[
            pltpu.VMEM((keys, WIDTH), BF16),
            pltpu.VMEM((keys, WIDTH), BF16),
            pltpu.VMEM((WIDTH, keys), BF16),
            pltpu.VMEM((keys, BLOCK), F32),
            pltpu.VMEM(((KEY_BLOCKS + 1) // 2 * 8, cols), F32),
            pltpu.VMEM((keys, cols), F32),
            pltpu.VMEM((keys, cols), F32),
            pltpu.VMEM((WIDTH, HEADS * BLOCK), F32),
            pltpu.VMEM((HEADS * BLOCK, WIDTH), BF16),
            pltpu.VMEM((HEADS * BLOCK, WIDTH), BF16),
            pltpu.VMEM((WIDTH, keys), BF16),
            pltpu.VMEM((keys, 2 * WIDTH), F32),
            pltpu.SMEM((1,), jnp.int32),
            pltpu.SMEM((KEY_BLOCKS + 1,), jnp.int32),
        ],
        compiler_params=pltpu.CompilerParams(vmem_limit_bytes=56 * 1024 * 1024),
    )(order, stripes, q, do, *kvs)


FIXED = 16
OTHERS = tuple(m for m in range(1, 32) if m != FIXED)


def plan_kernel(partner_ref, k_ref, v_ref, first_ref, second_ref, third_ref, order_ref, payload_ref):
    payload_ref[:, :WIDTH] = k_ref[...]
    payload_ref[:, WIDTH:] = v_ref[...]
    masks = [partner_ref[r, 0] for r in range(ROUNDS)]
    rest = [jnp.where(masks[r] == FIXED, masks[ROUNDS - 1], masks[r]) for r in range(ROUNDS - 1)]
    for ref, mask in zip((first_ref, second_ref, third_ref), rest):
        ref[0] = jnp.where(mask > FIXED, mask - 2, mask - 1)
    for r, mask in enumerate((0, FIXED, *rest)):
        order_ref[r] = mask


def plan(partner, key_rows, value_rows):
    vmem, smem = pl.BlockSpec(memory_space=pltpu.VMEM), pl.BlockSpec(memory_space=pltpu.SMEM)
    one = jax.ShapeDtypeStruct((1,), jnp.int32)
    return pl.pallas_call(
        plan_kernel,
        out_shape=[one, one, one, jax.ShapeDtypeStruct((ROUNDS + 1,), jnp.int32), jax.ShapeDtypeStruct((ROWS, 2 * WIDTH), BF16)],
        in_specs=[smem, vmem, vmem],
        out_specs=[smem] * 4 + [vmem],
    )(partner.T, key_rows, value_rows)


def finish_kernel(own, p1, p2, p3, p4, dk_ref, dv_ref):
    for ref, cols in ((dk_ref, slice(0, WIDTH)), (dv_ref, slice(WIDTH, 2 * WIDTH))):
        acc = own[:, cols]
        for p in (p1, p2, p3, p4):
            acc += p[:, cols].astype(F32)
        ref[...] = acc.astype(BF16)


def finish(own, parts):
    return pl.pallas_call(finish_kernel, out_shape=[jax.ShapeDtypeStruct((ROWS, WIDTH), BF16)] * 2)(own, *parts)


def swap_kernel(mask, mine, theirs, sent, came):
    partner = {"ctx": lax.axis_index("ctx") ^ mask}
    entered = pltpu.get_barrier_semaphore()
    pl.semaphore_signal(entered, inc=1, device_id=partner, device_id_type=MESH)
    pl.semaphore_wait(entered, 1)
    copy = pltpu.make_async_remote_copy(
        src_ref=mine, dst_ref=theirs, send_sem=sent, recv_sem=came, device_id=partner, device_id_type=MESH
    )
    copy.start()
    copy.wait()


def swap(mask, number, x):
    spec = pl.BlockSpec(memory_space=pl.ANY)
    return pl.pallas_call(
        functools.partial(swap_kernel, mask),
        out_shape=jax.ShapeDtypeStruct(x.shape, x.dtype),
        in_specs=[spec],
        out_specs=spec,
        scratch_shapes=[pltpu.SemaphoreType.DMA, pltpu.SemaphoreType.DMA],
        compiler_params=pltpu.CompilerParams(collective_id=number, has_side_effects=True),
    )(x)


def exchange(branch, arrays):
    fixed, *rest = arrays
    by = [functools.partial(swap, m, i) for i, m in enumerate(OTHERS)]
    across = lax.ppermute(fixed, "ctx", [(i, i ^ FIXED) for i in range(32)])
    return [across, *(lax.switch(b, by, x) for b, x in zip(branch, rest))]


def local(queries, key_rows, value_rows, out_grad, partner, stripes):
    *branch, order, payload = plan(partner, key_rows, value_rows)
    branch = [b.reshape(()) for b in branch]
    kvs = exchange(branch, (payload,) * ROUNDS)
    dq, own, *parts = attend(order, stripes, queries, out_grad, (payload, *kvs))
    return (dq, *finish(own, exchange(branch, parts)))


def solution(mesh):
    return jax.shard_map(
        local,
        mesh=mesh,
        in_specs=(P("ctx", "head"), P("ctx", "head"), P("ctx", "head"), P("ctx", "head"), P(), P()),
        out_specs=(P("ctx", "head"), P("ctx", "head"), P("ctx", "head")),
        check_vma=False,
    )
```
